32 devices in a mesh: dp: 4 (over z), expert: 8 (over y, x, core).
Axes of the slice: x: 2, y: 2, z: 4, core: 2. Of those that a mesh axis runs over, the one named last changes fastest.
Arguments:
- tokens: bfloat16 [512, 4096], P('dp'), may hold values from -6 to 6
- routes: int32 [512, 8], P('dp'), may hold values from 0 to 15, all different within a row; in each aligned block of 128 rows (0 to 127, 128 to 255, ...) at most 80 rows name the same one
- route_probs: float32 [512, 8], P('dp'), may hold values from 0.1 to 1
- w_gate: bfloat16 [16, 4096, 768], P('expert', 'dp'), may hold values from -0.09375 to 0.09375
- w_up: bfloat16 [16, 4096, 768], P('expert', 'dp'), may hold values from -0.09375 to 0.09375
- w_down: bfloat16 [16, 768, 4096], P('expert', None, 'dp'), may hold values from -0.21875 to 0.21875
- out_grad: bfloat16 [512, 4096], P('dp'), may hold values from -6 to 6
Outputs:
- mixed: bfloat16 [512, 4096], P('dp')
- input_grad: bfloat16 [512, 4096], P('dp')
- prob_grad: float32 [512, 8], P('dp')
- grad_gate: bfloat16 [16, 4096, 768], P('expert', 'dp')
- grad_up: bfloat16 [16, 4096, 768], P('expert', 'dp')
- grad_down: bfloat16 [16, 768, 4096], P('expert', None, 'dp')
The draws below stay inside these ranges and needn't reach their ends.
Inputs may be any that keep to these rules, and one draw needn't show every extreme that they name: `routes`: the ids in a row differ. In each group of 128 rows of one dp index no id is named by more than 80 rows, a bound that some block reaches.
All inputs are finite; a program needn't handle non-finite values.
Results may differ from the reference program's by a relative error of at most 0.02.
Values may be sent and summed in bfloat16 or wider, within the bound.
A program may use at most 128 MiB of HBM per device.

```python
import math
import jax
import jax.numpy as jnp
import numpy as np
from jax import lax

D = 4096
H = 768
TOP = 8
TOK_G = 128
EXPERTS = 16
CAP = 80
TOKENS = 512
N_DP = 4


def block_scale(own_key, extent, cuts, least, high):
    loudness, own = 1.0, jax.random.fold_in(own_key, 6)
    for axis_at, blocks in cuts:
        steps = jnp.exp(jax.random.uniform(jax.random.fold_in(own, axis_at), (blocks,), jnp.float32, least / len(cuts), high / len(cuts)))
        loudness = loudness * jnp.repeat(steps, extent[axis_at] // blocks).reshape([-1 if axis == axis_at else 1 for axis in range(len(extent))])
    return loudness


def routed_block(key, own, number, rows, number_of, top, most, slope):
    sequence = jax.random.permutation(key, number_of)
    packed, usual = load_shares(number_of, rows * top, most, slope, True), load_shares(number_of, rows * top, most, slope, False)
    places = jnp.arange(number_of)

    def named(sizes, offset_by):
        used = int((sizes > 0).sum())
        fixed = max(1, used // 4)
        moved = fixed + (places - fixed + offset_by * (used - fixed)) % max(1, number_of - fixed)
        return jnp.zeros((number_of,), jnp.int32).at[sequence[jnp.where(places < fixed, places, moved)]].set(jnp.asarray(sizes, jnp.int32))

    sizes = jnp.where(number % 4 == 0, named(packed, number // 4), named(usual, number - number // 4 - 1))
    mixed = jax.random.permutation(jax.random.fold_in(own, 3), number_of)
    donor, taker = mixed[0:number_of // 2 * 2:2], mixed[1:number_of // 2 * 2:2]
    slack = jnp.minimum(sizes[donor] - 1, most - sizes[taker]) // 2
    slack = jnp.where((donor == sequence[0]) | (taker == sequence[0]) | (sizes[taker] == 0), 0, jnp.maximum(slack, 0))
    moved = jax.random.randint(jax.random.fold_in(own, 4), (number_of // 2,), 0, 1 << 20) % (slack + 1)
    sizes = sizes.at[donor].add(-moved).at[taker].add(moved)
    labels = jnp.searchsorted(jnp.cumsum(sizes), jnp.arange(rows * top), side="right").astype(jnp.int32)
    grid = labels.reshape(top, rows).T
    grid = grid[jax.random.permutation(jax.random.fold_in(own, 1), rows)]
    offset_by = jax.random.randint(jax.random.fold_in(own, 2), (rows, 1), 0, top)
    return jnp.take_along_axis(grid, (jnp.arange(top)[None, :] + offset_by) % top, axis=1)


def load_shares(number_of, total, bound, slope, full):
    weights = [(1 << 20) // math.isqrt(standing ** slope) + 1 for standing in range(1, number_of + 1)]
    largest = bound if full else min(bound, max(-(-total // number_of), total * weights[0] // sum(weights)))
    least = 1 if total - largest >= number_of - 1 else 0
    counts, surplus = [largest] + [least] * (number_of - 1), total - largest - least * (number_of - 1)
    while surplus > 0:
        free = [i for i in range(1, number_of) if counts[i] < largest] or [i for i in range(1, number_of) if counts[i] < bound]
        whole, left = sum([weights[i] for i in free]), surplus
        for i in free:
            extra = min(bound - counts[i], max(1, left * weights[i] // whole), surplus)
            counts[i] = counts[i] + extra
            surplus = surplus - extra
    return np.array(counts)


def noise(own_key, shape, scale, most, cuts=(), held_as=jnp.bfloat16):
    values = scale * jax.random.normal(own_key, shape, jnp.float32)
    if cuts:
        values = values * block_scale(own_key, shape, cuts, -0.22, 0.18)
    return jnp.clip(values, -most, most).astype(held_as)


def setup_inputs(seed: int = 0) -> dict:
    key_list = jax.random.split(jax.random.key(seed), 8)
    tokens = noise(key_list[0], (TOKENS, D), 1.0, 6.0, ((0, 4),))
    routes_keys = jax.random.split(jax.random.fold_in(key_list[1], 1), TOKENS // TOK_G)
    routes_turns = jax.random.permutation(jax.random.fold_in(key_list[1], 3), TOKENS // TOK_G)
    routes = jax.vmap(lambda own, number: routed_block(jax.random.fold_in(key_list[1], 2), own, number, TOK_G, EXPERTS, TOP, CAP, 2))(routes_keys, routes_turns).reshape((TOKENS, TOP))
    route_probs = jnp.clip(jnp.exp(math.log(1.0) - 2.3025851 * jax.random.uniform(key_list[2], (TOKENS, TOP), jnp.float32) ** block_scale(key_list[2], (TOKENS, TOP), ((0, 4),), -0.2, 0.2)), 0.1, 1.0)
    w_gate = noise(key_list[3], (EXPERTS, D, H), D ** -0.5, 0.09375, ((0, 8), (1, 4)))
    w_up = noise(key_list[4], (EXPERTS, D, H), D ** -0.5, 0.09375, ((0, 8), (1, 4)))
    w_down = noise(key_list[5], (EXPERTS, H, D), H ** -0.5, 0.21875, ((0, 8), (2, 4)))
    out_grad = noise(key_list[6], (TOKENS, D), 1.0, 6.0, ((0, 4),))
    return dict(tokens=tokens, routes=routes, route_probs=route_probs, w_gate=w_gate, w_up=w_up, w_down=w_down, out_grad=out_grad)


def group_tables(route_group, prob_group):
    flat_ids = route_group.reshape(-1)
    onehot = (flat_ids[:, None] == jnp.arange(EXPERTS, dtype=jnp.int32)[None, :]).astype(jnp.int32)
    slot_rank = jnp.sum((jnp.cumsum(onehot, 0) - onehot) * onehot, 1)
    target = flat_ids * CAP + slot_rank
    select = (jnp.arange(EXPERTS * CAP, dtype=jnp.int32)[:, None] == target[None, :]).astype(jnp.float32)
    per_token = jnp.sum(select.reshape(EXPERTS * CAP, TOK_G, TOP), 2)
    weights = jnp.dot(select, prob_group.reshape(-1), precision=lax.Precision.HIGHEST)
    return select, per_token, weights


def slice_sum(left, right):
    rows_n = left.shape[0]
    left_blocks = left.astype(jnp.float32).reshape(rows_n, N_DP, D // N_DP)
    right_blocks = right.astype(jnp.float32).reshape(N_DP, D // N_DP, right.shape[1])
    parts = jnp.einsum("rsd,sdh->srh", left_blocks, right_blocks, precision=lax.Precision.HIGHEST)
    rounded = lax.optimization_barrier(parts.astype(jnp.bfloat16))
    return jnp.sum(rounded.astype(jnp.float32), 0)


def expert_pass(inputs):
    rows, grads, gate_w, up_w, down_w = inputs
    gate_sum = slice_sum(rows, gate_w)
    up_sum = slice_sum(rows, up_w)
    back_sum = slice_sum(grads, down_w.T)
    gate_sig = jax.nn.sigmoid(gate_sum)
    activated = gate_sum * gate_sig
    hidden_rows = (activated * up_sum).astype(jnp.bfloat16)
    delta_gate = (back_sum * up_sum * gate_sig * (1.0 + gate_sum * (1.0 - gate_sig))).astype(jnp.bfloat16)
    delta_up = (back_sum * activated).astype(jnp.bfloat16)
    expert_out = jnp.dot(hidden_rows, down_w, preferred_element_type=jnp.float32).astype(jnp.bfloat16)
    input_rows = (jnp.dot(delta_gate, gate_w.T, preferred_element_type=jnp.float32)
                  + jnp.dot(delta_up, up_w.T, preferred_element_type=jnp.float32)).astype(jnp.bfloat16)
    grad_down = jnp.dot(hidden_rows.T, grads, preferred_element_type=jnp.float32).astype(jnp.bfloat16)
    grad_gate = jnp.dot(rows.T, delta_gate, preferred_element_type=jnp.float32).astype(jnp.bfloat16)
    grad_up = jnp.dot(rows.T, delta_up, preferred_element_type=jnp.float32).astype(jnp.bfloat16)
    return expert_out, input_rows, grad_gate, grad_up, grad_down


def by_expert(values):
    return values.reshape(N_DP, EXPERTS, CAP, D).transpose(1, 0, 2, 3).reshape(EXPERTS, N_DP * CAP, D)


def by_group(values):
    return values.reshape(EXPERTS, N_DP, CAP, D).transpose(1, 0, 2, 3).reshape(N_DP, EXPERTS * CAP, D)


def reference(tokens, routes, route_probs, w_gate, w_up, w_down, out_grad):
    select, per_token, weights = jax.vmap(group_tables)(routes.reshape(N_DP, TOK_G, TOP), route_probs.reshape(N_DP, TOK_G, TOP))
    token_groups = tokens.reshape(N_DP, TOK_G, D).astype(jnp.float32)
    grad_groups = out_grad.reshape(N_DP, TOK_G, D).astype(jnp.float32)
    sent_rows = jnp.einsum("gst,gtd->gsd", per_token, token_groups, precision=lax.Precision.HIGHEST).astype(jnp.bfloat16)
    slot_grad = jnp.einsum("gst,gtd->gsd", per_token, grad_groups, precision=lax.Precision.HIGHEST)
    weighted = (weights[:, :, None] * slot_grad).astype(jnp.bfloat16)
    expert_out, input_rows, grad_gate, grad_up, grad_down = lax.map(
        expert_pass, (by_expert(sent_rows), by_expert(weighted), w_gate, w_up, w_down))
    out_groups = by_group(expert_out).astype(jnp.float32)
    input_groups = by_group(input_rows).astype(jnp.float32)
    mixed = jnp.einsum("gst,gsd->gtd", per_token * weights[:, :, None], out_groups, precision=lax.Precision.HIGHEST)
    input_sum = jnp.einsum("gst,gsd->gtd", per_token, input_groups, precision=lax.Precision.HIGHEST)
    scores = jnp.sum(slot_grad * out_groups, 2)
    prob_grad = jnp.einsum("gsk,gs->gk", select, scores, precision=lax.Precision.HIGHEST)
    return (mixed.reshape(TOKENS, D).astype(jnp.bfloat16), input_sum.reshape(TOKENS, D).astype(jnp.bfloat16),
            prob_grad.reshape(TOKENS, TOP), grad_gate, grad_up, grad_down)
```

```python
import jax
import jax.numpy as jnp
from jax import lax
from jax.experimental import pallas as pl
from jax.experimental.pallas import tpu as pltpu
from jax.sharding import PartitionSpec as P


def plain_shards(tokens, routes, route_probs, w_gate, w_up, w_down, out_grad):
    tok_g, fan_out = routes.shape
    exp_dev, slice_d, hidden = w_gate.shape
    experts = exp_dev * lax.axis_size("expert")
    capacity = min(tok_g, max(2, 5 * tok_g * fan_out // (4 * experts)))
    slot_count = exp_dev * capacity
    owner_index = lax.axis_index("expert")
    flat_ids = routes.reshape(-1)
    onehot = (flat_ids[:, None] == jnp.arange(experts, dtype=jnp.int32)[None, :]).astype(jnp.int32)
    slot_rank = jnp.sum((jnp.cumsum(onehot, 0) - onehot) * onehot, 1)
    local_id = flat_ids - owner_index * exp_dev
    target = jnp.where((local_id >= 0) & (local_id < exp_dev), local_id * capacity + slot_rank, -1)
    select = (jnp.arange(slot_count, dtype=jnp.int32)[:, None] == target[None, :]).astype(
        jnp.float32
    )
    per_token = jnp.sum(select.reshape(slot_count, tok_g, fan_out), 2)
    weights = jnp.dot(select, route_probs.reshape(-1), precision=lax.Precision.HIGHEST)
    token_pick = per_token.astype(jnp.bfloat16)
    sent_rows = jnp.dot(token_pick, tokens, preferred_element_type=jnp.float32).astype(jnp.bfloat16)
    grad_rows = jnp.dot(token_pick, out_grad, preferred_element_type=jnp.float32)
    grad_sent = (weights[:, None] * grad_rows).astype(jnp.bfloat16)
    all_rows, all_grads = (
        lax.all_to_all(sent_rows, "dp", split_axis=1, concat_axis=0, tiled=True),
        lax.all_to_all(grad_sent, "dp", split_axis=1, concat_axis=0, tiled=True),
    )
    groups = all_rows.shape[0] // slot_count
    part_rows = all_rows.reshape(
        slot_count * lax.axis_size("dp") // slot_count, exp_dev, capacity, slice_d
    )
    part_grads = all_grads.reshape(
        slot_count * lax.axis_size("dp") // slot_count, exp_dev, capacity, slice_d
    )
    gate_part = jnp.einsum("secd,edh->sech", part_rows, w_gate, preferred_element_type=jnp.float32)
    up_part = jnp.einsum("secd,edh->sech", part_rows, w_up, preferred_element_type=jnp.float32)
    back_part = jnp.einsum("secd,ehd->sech", part_grads, w_down, preferred_element_type=jnp.float32)
    reduced = lax.psum_scatter(
        jnp.concatenate([gate_part, up_part, back_part], 3)
        .reshape(slot_count * lax.axis_size("dp"), 3 * hidden)
        .astype(jnp.bfloat16),
        "dp",
        scatter_dimension=0,
        tiled=True,
    ).astype(jnp.float32)
    gate_sum = reduced[:, :hidden]
    up_sum = reduced[:, hidden : 2 * hidden]
    back_sum = reduced[:, 2 * hidden :]
    gate_sig = jax.nn.sigmoid(gate_sum)
    activated = gate_sum * gate_sig
    hidden_rows = (activated * up_sum).astype(jnp.bfloat16)
    delta_gate = (back_sum * up_sum * gate_sig * (1.0 + gate_sum * (1.0 - gate_sig))).astype(
        jnp.bfloat16
    )
    delta_up = (back_sum * activated).astype(jnp.bfloat16)
    all_hidden, all_delta = (
        lax.all_gather(hidden_rows, "dp", axis=0, tiled=True),
        lax.all_gather(jnp.concatenate([delta_gate, delta_up], 1), "dp", axis=0, tiled=True),
    )
    hidden_four = all_hidden.reshape(groups, exp_dev, capacity, hidden)
    delta_four = all_delta.reshape(groups, exp_dev, capacity, 2 * hidden)
    rows_four = all_rows.reshape(groups, exp_dev, capacity, slice_d)
    grads_four = all_grads.reshape(groups, exp_dev, capacity, slice_d)
    gate_delta = delta_four[..., :hidden]
    up_delta = delta_four[..., hidden:]
    expert_out = jnp.einsum(
        "sech,ehd->secd", hidden_four, w_down, preferred_element_type=jnp.float32
    )
    expert_out = expert_out.astype(jnp.bfloat16).reshape(groups * slot_count, slice_d)
    input_part = jnp.einsum(
        "sech,edh->secd", gate_delta, w_gate, preferred_element_type=jnp.float32
    ) + jnp.einsum("sech,edh->secd", up_delta, w_up, preferred_element_type=jnp.float32)
    input_part = input_part.astype(jnp.bfloat16).reshape(groups * slot_count, slice_d)
    grad_down = jnp.einsum(
        "sech,secd->ehd", hidden_four, grads_four, preferred_element_type=jnp.float32
    ).astype(jnp.bfloat16)
    grad_gate = jnp.einsum(
        "secd,sech->edh", rows_four, gate_delta, preferred_element_type=jnp.float32
    ).astype(jnp.bfloat16)
    grad_up = jnp.einsum(
        "secd,sech->edh", rows_four, up_delta, preferred_element_type=jnp.float32
    ).astype(jnp.bfloat16)
    out_rows, input_rows = (
        lax.all_to_all(expert_out, "dp", split_axis=0, concat_axis=1, tiled=True),
        lax.all_to_all(input_part, "dp", split_axis=0, concat_axis=1, tiled=True),
    )
    out_float = out_rows.astype(jnp.float32)
    scores = jnp.sum(grad_rows * out_float, 1)
    prob_part = jnp.dot(select.T, scores, precision=lax.Precision.HIGHEST).reshape(tok_g, fan_out)
    mix_table = (per_token * weights[:, None]).T
    mixed_part = jnp.dot(mix_table, out_float, precision=lax.Precision.HIGHEST)
    input_sum = jnp.dot(token_pick.T, input_rows, preferred_element_type=jnp.float32)
    mixed_block, input_block = (
        lax.psum_scatter(
            mixed_part.astype(jnp.bfloat16), "expert", scatter_dimension=1, tiled=True
        ).astype(jnp.float32),
        lax.psum_scatter(
            input_sum.astype(jnp.bfloat16), "expert", scatter_dimension=1, tiled=True
        ).astype(jnp.float32),
    )
    mixed, input_grad = (
        lax.all_gather(mixed_block.astype(jnp.bfloat16), "expert", axis=1, tiled=True),
        lax.all_gather(input_block.astype(jnp.bfloat16), "expert", axis=1, tiled=True),
    )
    prob_grad = lax.psum(prob_part, "expert")
    return (mixed, input_grad, prob_grad, grad_gate, grad_up, grad_down)


MESH = pl.DeviceIdType.MESH
F32, BF16 = jnp.float32, jnp.bfloat16
DP, EP = 4, 8
ROWS = 32


def place():
    z, e = lax.axis_index("dp"), lax.axis_index("expert")
    core, chip = lax.rem(e, 2), lax.div(e, 2)
    x, y = lax.rem(chip, 2), lax.div(chip, 2)
    across = [y * 2 + (1 - x), (1 - y) * 2 + x, (1 - y) * 2 + (1 - x)]
    return z, e, core, chip, across


def lanes(start, size):
    return pl.ds(pl.multiple_of(start, 128), size)


def rows_at(start, size):
    return pl.ds(pl.multiple_of(start, 32), size)


def greet(peers):
    barrier = pltpu.get_barrier_semaphore()
    for peer in peers:
        pl.semaphore_signal(barrier, inc=1, device_id=peer, device_id_type=MESH)
    pl.semaphore_wait(barrier, len(peers))


def push(src, dst, send, recv, peer):
    return pltpu.make_async_remote_copy(
        src_ref=src, dst_ref=dst, send_sem=send, recv_sem=recv, device_id=peer, device_id_type=MESH
    )


def spread_kernel(tok, grad, info, both, infos, s1, r1, s2, r2, s3, r3):
    z, e, core, chip, across = place()
    tok_g, total = tok.shape[0], tok.shape[0] * DP
    block = tok.shape[1] // DP
    part = block // EP
    sibling = chip * 2 + (1 - core)
    peers = [(lax.rem(z + k, DP), e) for k in (1, 2, 3)]
    greet(peers + [(z, sibling)] + [(z, c * 2 + core) for c in across])
    mine = lanes(e * part, part)
    sent, first = [], []
    for k, peer in enumerate(peers):
        for a, src in enumerate((tok, grad)):
            first.append(
                push(
                    src.at[:, lanes(peer[0] * block + e * part, part)],
                    both.at[rows_at(a * total + z * tok_g, tok_g), mine],
                    s1.at[a, k],
                    r1.at[a, k],
                    peer,
                )
            )
        first.append(push(info, infos.at[z], s1.at[2, k], r1.at[2, k], peer))
    for copy in first:
        copy.start()
    for a, src in enumerate((tok, grad)):
        both[rows_at(a * total + z * tok_g, tok_g), mine] = src[
            :, lanes(z * block + e * part, part)
        ]
    infos[z] = info[...]
    for copy in first:
        copy.wait_recv()
    second = [
        push(both.at[:, mine], both.at[:, mine], s2.at[j], r2.at[j], (z, c * 2 + core))
        for j, c in enumerate(across)
    ]
    for copy in second:
        copy.start()
    third = [push(both.at[:, mine], both.at[:, mine], s3.at[0], r3.at[0], (z, sibling))]
    third[0].start()
    for j, c in enumerate(across):
        second[j].wait_recv()
        theirs = lanes((c * 2 + core) * part, part)
        third.append(
            push(
                both.at[:, theirs], both.at[:, theirs], s3.at[j + 1], r3.at[j + 1], (z, sibling)
            )
        )
        third[-1].start()
    for copy in third:
        copy.wait_recv()
    for copy in first + second + third:
        copy.wait_send()


def hidden_kernel(part, out, got, summed, s1, r1, s2, r2):
    z, e = lax.axis_index("dp"), lax.axis_index("expert")
    half = part.shape[0] // 2
    width = part.shape[1] // 3
    steps = half // ROWS
    barrier = pltpu.get_barrier_semaphore()
    inner = (z > 0) & (z < DP - 1)

    @pl.when(z > 0)
    def _():
        pl.semaphore_signal(barrier, inc=1, device_id=(z - 1, e), device_id_type=MESH)

    @pl.when(z < DP - 1)
    def _():
        pl.semaphore_signal(barrier, inc=1, device_id=(z + 1, e), device_id_type=MESH)

    @pl.when(inner)
    def _():
        pl.semaphore_wait(barrier, 2)

    @pl.when(jnp.logical_not(inner))
    def _():
        pl.semaphore_wait(barrier, 1)

    def onward(d):
        return (z + 1, e) if d == 0 else (z - 1, e)

    def backward(d):
        return (z - 1, e) if d == 0 else (z + 1, e)

    def spot(d, c):
        return rows_at(d * half + c * ROWS, ROWS)

    def fan_in(d, c, src):
        return push(src, got.at[d, c], s1.at[d, c], r1.at[d, c], onward(d))

    def fan_out(d, c):
        rows = spot(d, c)
        return push(out.at[rows], out.at[rows], s2.at[d, c], r2.at[d, c], backward(d))

    first = [z == 0, z == DP - 1]
    last = [z == DP - 1, z == 0]

    def feed(c, carry):
        for d in (0, 1):

            @pl.when(first[d])
            def _():
                fan_in(d, c, part.at[spot(d, c)]).start()

        return carry

    lax.fori_loop(0, steps, feed, 0)

    def gather(c, carry):
        for d in (0, 1):

            @pl.when(inner)
            def _():
                fan_in(d, c, summed.at[d, c]).wait_recv()
                total = got[d, c].astype(F32) + part[spot(d, c), :].astype(F32)
                summed[d, c] = total.astype(BF16)
                fan_in(d, c, summed.at[d, c]).start()

            @pl.when(last[d])
            def _():
                fan_in(d, c, summed.at[d, c]).wait_recv()
                total = got[d, c].astype(F32) + part[spot(d, c), :].astype(F32)
                gate = total[:, :width]
                up = total[:, width : 2 * width]
                back = total[:, 2 * width :]
                sig = jax.nn.sigmoid(gate)
                act = gate * sig
                rows = spot(d, c)
                out[rows, 0:width] = (act * up).astype(BF16)
                out[rows, width : 2 * width] = (
                    back * up * sig * (1.0 + gate * (1.0 - sig))
                ).astype(BF16)
                out[rows, 2 * width : 3 * width] = (back * act).astype(BF16)
                fan_out(d, c).start()

        return carry

    lax.fori_loop(0, steps, gather, 0)

    def relay(c, carry):
        for d in (0, 1):

            @pl.when(inner)
            def _():
                fan_out(d, c).wait_recv()
                fan_out(d, c).start()

        return carry

    lax.fori_loop(0, steps, relay, 0)

    def finish(c, carry):
        for d in (0, 1):

            @pl.when(first[d])
            def _():
                fan_out(d, c).wait_recv()
                fan_in(d, c, part.at[spot(d, c)]).wait_send()

            @pl.when(inner)
            def _():
                fan_in(d, c, summed.at[d, c]).wait_send()
                fan_out(d, c).wait_send()

            @pl.when(last[d])
            def _():
                fan_out(d, c).wait_send()

        return carry

    lax.fori_loop(0, steps, finish, 0)


def collect_kernel(
    part, prob_part, mixed, inp, prob, near, sums, far, own, table, zprob, eprob,
    s1, r1, s2, r2, s3, r3, s4, r4, s5, r5, s6, r6, s7, r7,
):
    z, e, core, chip, across = place()
    tok_g, total = mixed.shape[0], mixed.shape[0] * DP
    block = part.shape[1]
    width = block // EP
    sibling = chip * 2 + (1 - core)
    zpeers = [(lax.rem(z + k, DP), e) for k in (1, 2, 3)]
    epeers = [(z, lax.rem(e + i, EP)) for i in range(1, EP)]
    greet(zpeers + epeers)
    done = []
    near_in = []
    order = across + [chip]
    for i, c in enumerate(order):
        copy = push(
            part.at[:, lanes((c * 2 + 1 - core) * width, width)],
            near.at[c],
            s1.at[i],
            r1.at[i],
            (z, sibling),
        )
        copy.start()
        near_in.append(copy)
    prob_in = []
    for k, peer in enumerate(zpeers):
        copy = push(prob_part.at[peer[0]], zprob.at[k], s6.at[k], r6.at[k], peer)
        copy.start()
        prob_in.append(copy)
    far_in = []
    for i, c in enumerate(across):
        near_in[i].wait_recv()
        sums[c] = (
            part[:, lanes((c * 2 + core) * width, width)].astype(F32) + near[c].astype(F32)
        ).astype(BF16)
        copy = push(sums.at[c], far.at[i], s2.at[i], r2.at[i], (z, c * 2 + core))
        copy.start()
        far_in.append(copy)
    for copy in prob_in:
        copy.wait_recv()
    eprob[e] = prob_part[z] + zprob[0] + zprob[1] + zprob[2]
    prob_out = []
    for i, peer in enumerate(epeers):
        copy = push(eprob.at[e], eprob.at[e], s7.at[i], r7.at[i], peer)
        copy.start()
        prob_out.append(copy)
    near_in[3].wait_recv()
    for copy in far_in:
        copy.wait_recv()
    own[...] = (
        part[:, lanes(e * width, width)].astype(F32)
        + near[chip].astype(F32)
        + far[0].astype(F32)
        + far[1].astype(F32)
        + far[2].astype(F32)
    ).astype(BF16)
    home = []
    for k, peer in enumerate(zpeers):
        for a in (0, 1):
            copy = push(
                own.at[rows_at(a * total + peer[0] * tok_g, tok_g)],
                table.at[e, pl.ds(a * tok_g, tok_g), lanes(z * width, width)],
                s3.at[a, k],
                r3.at[a, k],
                peer,
            )
            copy.start()
            home.append(copy)
    for a in (0, 1):
        table[e, pl.ds(a * tok_g, tok_g), lanes(z * width, width)] = own[
            rows_at(a * total + z * tok_g, tok_g)
        ]
    for copy in home:
        copy.wait_recv()
    wide = [
        push(table.at[e], table.at[e], s4.at[i], r4.at[i], (z, c * 2 + core))
        for i, c in enumerate(across)
    ]
    pair = [push(table.at[e], table.at[e], s5.at[0], r5.at[0], (z, sibling))]
    for copy in wide + pair:
        copy.start()
    for i, c in enumerate(across):
        wide[i].wait_recv()
        there = c * 2 + core
        copy = push(table.at[there], table.at[there], s5.at[i + 1], r5.at[i + 1], (z, sibling))
        copy.start()
        pair.append(copy)
    for copy in prob_out:
        copy.wait_recv()
    prob[...] = jnp.sum(eprob[...], axis=0)
    for copy in pair:
        copy.wait_recv()
    for q in range(EP):
        for b in range(DP):
            at = slice(b * block + q * width, b * block + (q + 1) * width)
            mixed[:, at] = table[q, 0:tok_g, b * width : (b + 1) * width]
            inp[:, at] = table[q, tok_g : 2 * tok_g, b * width : (b + 1) * width]
    for copy in near_in + prob_in + far_in + prob_out + home + wide + pair:
        copy.wait_send()


def vmem():
    return pl.BlockSpec(memory_space=pltpu.VMEM)


def sems(*shapes):
    return [pltpu.SemaphoreType.DMA(s) for s in shapes for _ in (0, 1)]


def params(number):
    return pltpu.CompilerParams(
        collective_id=number, has_side_effects=True, vmem_limit_bytes=40 * 2**20
    )


def shards(tokens, routes, route_probs, w_gate, w_up, w_down, out_grad):
    tok_g, fan_out = routes.shape
    exp_dev, slice_d, hidden = w_gate.shape
    experts = exp_dev * EP
    capacity = min(tok_g, max(2, 5 * tok_g * fan_out // (4 * experts)))
    total, feats = tok_g * DP, tokens.shape[1]
    owner = lax.axis_index("expert")
    info = jnp.concatenate([routes.astype(F32), route_probs], 1).T
    both, infos = pl.pallas_call(
        spread_kernel,
        out_shape=(
            jax.ShapeDtypeStruct((2 * total, slice_d), BF16),
            jax.ShapeDtypeStruct((DP,) + info.shape, F32),
        ),
        in_specs=[vmem()] * 3,
        out_specs=(vmem(), vmem()),
        scratch_shapes=sems((3, 3), (3,), (4,)),
        compiler_params=params(0),
        name="spread",
    )(tokens, out_grad, info)
    ids = infos[:, :fan_out].astype(jnp.int32)
    probs = infos[:, fan_out:]
    local = owner * exp_dev + jnp.arange(exp_dev, dtype=jnp.int32)
    named = (ids[None] == local[:, None, None, None]).astype(F32)
    member = jnp.sum(named, 2)
    weight = jnp.sum(named * probs[None], 2)
    earlier = jnp.arange(tok_g)[:, None] < jnp.arange(tok_g)[None, :]
    rank = jnp.einsum(
        "egt,tu->egu", member.astype(BF16), earlier.astype(BF16), preferred_element_type=F32
    )
    chosen = (rank[:, :, None, :] == jnp.arange(capacity, dtype=F32)[:, None]) & (
        member[:, :, None, :] > 0
    )
    pick = chosen.astype(BF16)
    slot_weight = jnp.sum(jnp.where(chosen, weight[:, :, None, :], 0.0), 3)
    parts = both.reshape(2, DP, tok_g, slice_d)
    rows = jnp.einsum("egct,gtd->egcd", pick, parts[0], preferred_element_type=F32)
    rows = rows.astype(BF16).reshape(exp_dev, DP * capacity, slice_d)
    grad_rows = jnp.einsum("egct,gtd->egcd", pick, parts[1], preferred_element_type=F32)
    grads = (slot_weight[..., None] * grad_rows).astype(BF16)
    grads = grads.reshape(exp_dev, DP * capacity, slice_d)
    gate_part = jnp.einsum("erd,edh->erh", rows, w_gate, preferred_element_type=F32)
    up_part = jnp.einsum("erd,edh->erh", rows, w_up, preferred_element_type=F32)
    back_part = jnp.einsum("erd,ehd->erh", grads, w_down, preferred_element_type=F32)
    part = jnp.concatenate(
        [gate_part.astype(BF16), up_part.astype(BF16), back_part.astype(BF16)], 2
    ).reshape(exp_dev * DP * capacity, 3 * hidden)
    steps = part.shape[0] // 2 // ROWS
    full = pl.pallas_call(
        hidden_kernel,
        out_shape=jax.ShapeDtypeStruct(part.shape, BF16),
        in_specs=[vmem()],
        out_specs=vmem(),
        scratch_shapes=[
            pltpu.VMEM((2, steps, ROWS, 3 * hidden), BF16),
            pltpu.VMEM((2, steps, ROWS, 3 * hidden), BF16),
        ]
        + sems((2, steps), (2, steps)),
        compiler_params=params(1),
        name="hidden",
    )(part)
    full = full.reshape(exp_dev, DP * capacity, 3 * hidden)
    hid = full[..., :hidden]
    d_gate = full[..., hidden : 2 * hidden]
    d_up = full[..., 2 * hidden :]
    outs = jnp.einsum("erh,ehd->erd", hid, w_down, preferred_element_type=F32)
    outs = outs.reshape(exp_dev, DP, capacity, slice_d)
    inputs = jnp.einsum("erh,edh->erd", d_gate, w_gate, preferred_element_type=F32) + jnp.einsum(
        "erh,edh->erd", d_up, w_up, preferred_element_type=F32
    )
    inputs = inputs.astype(BF16).reshape(exp_dev, DP, capacity, slice_d)
    scores = jnp.sum(grad_rows * outs, 3)
    by_token = jnp.sum(jnp.where(chosen, scores[..., None], 0.0), 2)
    prob_part = jnp.sum(named * by_token[:, :, None, :], 0)
    scaled = (slot_weight[..., None] * outs).astype(BF16)
    mixed_part = jnp.einsum("egct,egcd->gtd", pick, scaled, preferred_element_type=F32)
    input_sum = jnp.einsum("egct,egcd->gtd", pick, inputs, preferred_element_type=F32)
    packed = jnp.concatenate([mixed_part.astype(BF16), input_sum.astype(BF16)], 0)
    packed = packed.reshape(2 * total, slice_d)
    width = slice_d // EP
    mixed, input_grad, prob = pl.pallas_call(
        collect_kernel,
        out_shape=(
            jax.ShapeDtypeStruct((tok_g, feats), BF16),
            jax.ShapeDtypeStruct((tok_g, feats), BF16),
            jax.ShapeDtypeStruct((fan_out, tok_g), F32),
        ),
        in_specs=[vmem()] * 2,
        out_specs=(vmem(), vmem(), vmem()),
        scratch_shapes=[
            pltpu.VMEM((4, 2 * total, width), BF16),
            pltpu.VMEM((4, 2 * total, width), BF16),
            pltpu.VMEM((3, 2 * total, width), BF16),
            pltpu.VMEM((2 * total, width), BF16),
            pltpu.VMEM((EP, 2 * tok_g, DP * width), BF16),
            pltpu.VMEM((3, fan_out, tok_g), F32),
            pltpu.VMEM((EP, fan_out, tok_g), F32),
        ]
        + sems((4,), (3,), (2, 3), (3,), (4,), (3,), (7,)),
        compiler_params=params(2),
        name="collect",
    )(packed, prob_part)
    grad_down = jnp.einsum("erh,erd->ehd", hid, grads, preferred_element_type=F32).astype(BF16)
    grad_gate = jnp.einsum("erd,erh->edh", rows, d_gate, preferred_element_type=F32).astype(BF16)
    grad_up = jnp.einsum("erd,erh->edh", rows, d_up, preferred_element_type=F32).astype(BF16)
    return (mixed, input_grad, prob.T, grad_gate, grad_up, grad_down)


def solution(mesh):
    in_specs = (
        P("dp", None),
        P("dp", None),
        P("dp", None),
        P("expert", "dp", None),
        P("expert", "dp", None),
        P("expert", None, "dp"),
        P("dp", None),
    )
    out_specs = (
        P("dp", None),
        P("dp", None),
        P("dp", None),
        P("expert", "dp", None),
        P("expert", "dp", None),
        P("expert", None, "dp"),
    )
    body = shards if (mesh.shape["dp"], mesh.shape["expert"]) == (DP, EP) else plain_shards
    return jax.shard_map(body, mesh=mesh, in_specs=in_specs, out_specs=out_specs, check_vma=False)
```

```python
import jax
import jax.numpy as jnp
from jax import lax
from jax.experimental import pallas as pl
from jax.experimental.pallas import tpu as pltpu
from jax.sharding import PartitionSpec as P


def plain_shards(tokens, routes, route_probs, w_gate, w_up, w_down, out_grad):
    tok_g, fan_out = routes.shape
    exp_dev, slice_d, hidden = w_gate.shape
    experts = exp_dev * lax.axis_size("expert")
    capacity = min(tok_g, max(2, 5 * tok_g * fan_out // (4 * experts)))
    slot_count = exp_dev * capacity
    owner_index = lax.axis_index("expert")
    flat_ids = routes.reshape(-1)
    onehot = (flat_ids[:, None] == jnp.arange(experts, dtype=jnp.int32)[None, :]).astype(jnp.int32)
    slot_rank = jnp.sum((jnp.cumsum(onehot, 0) - onehot) * onehot, 1)
    local_id = flat_ids - owner_index * exp_dev
    target = jnp.where((local_id >= 0) & (local_id < exp_dev), local_id * capacity + slot_rank, -1)
    select = (jnp.arange(slot_count, dtype=jnp.int32)[:, None] == target[None, :]).astype(
        jnp.float32
    )
    per_token = jnp.sum(select.reshape(slot_count, tok_g, fan_out), 2)
    weights = jnp.dot(select, route_probs.reshape(-1), precision=lax.Precision.HIGHEST)
    token_pick = per_token.astype(jnp.bfloat16)
    sent_rows = jnp.dot(token_pick, tokens, preferred_element_type=jnp.float32).astype(jnp.bfloat16)
    grad_rows = jnp.dot(token_pick, out_grad, preferred_element_type=jnp.float32)
    grad_sent = (weights[:, None] * grad_rows).astype(jnp.bfloat16)
    all_rows, all_grads = (
        lax.all_to_all(sent_rows, "dp", split_axis=1, concat_axis=0, tiled=True),
        lax.all_to_all(grad_sent, "dp", split_axis=1, concat_axis=0, tiled=True),
    )
    groups = all_rows.shape[0] // slot_count
    part_rows = all_rows.reshape(
        slot_count * lax.axis_size("dp") // slot_count, exp_dev, capacity, slice_d
    )
    part_grads = all_grads.reshape(
        slot_count * lax.axis_size("dp") // slot_count, exp_dev, capacity, slice_d
    )
    gate_part = jnp.einsum("secd,edh->sech", part_rows, w_gate, preferred_element_type=jnp.float32)
    up_part = jnp.einsum("secd,edh->sech", part_rows, w_up, preferred_element_type=jnp.float32)
    back_part = jnp.einsum("secd,ehd->sech", part_grads, w_down, preferred_element_type=jnp.float32)
    reduced = lax.psum_scatter(
        jnp.concatenate([gate_part, up_part, back_part], 3)
        .reshape(slot_count * lax.axis_size("dp"), 3 * hidden)
        .astype(jnp.bfloat16),
        "dp",
        scatter_dimension=0,
        tiled=True,
    ).astype(jnp.float32)
    gate_sum = reduced[:, :hidden]
    up_sum = reduced[:, hidden : 2 * hidden]
    back_sum = reduced[:, 2 * hidden :]
    gate_sig = jax.nn.sigmoid(gate_sum)
    activated = gate_sum * gate_sig
    hidden_rows = (activated * up_sum).astype(jnp.bfloat16)
    delta_gate = (back_sum * up_sum * gate_sig * (1.0 + gate_sum * (1.0 - gate_sig))).astype(
        jnp.bfloat16
    )
    delta_up = (back_sum * activated).astype(jnp.bfloat16)
    all_hidden, all_delta = (
        lax.all_gather(hidden_rows, "dp", axis=0, tiled=True),
        lax.all_gather(jnp.concatenate([delta_gate, delta_up], 1), "dp", axis=0, tiled=True),
    )
    hidden_four = all_hidden.reshape(groups, exp_dev, capacity, hidden)
    delta_four = all_delta.reshape(groups, exp_dev, capacity, 2 * hidden)
    rows_four = all_rows.reshape(groups, exp_dev, capacity, slice_d)
    grads_four = all_grads.reshape(groups, exp_dev, capacity, slice_d)
    gate_delta = delta_four[..., :hidden]
    up_delta = delta_four[..., hidden:]
    expert_out = jnp.einsum(
        "sech,ehd->secd", hidden_four, w_down, preferred_element_type=jnp.float32
    )
    expert_out = expert_out.astype(jnp.bfloat16).reshape(groups * slot_count, slice_d)
    input_part = jnp.einsum(
        "sech,edh->secd", gate_delta, w_gate, preferred_element_type=jnp.float32
    ) + jnp.einsum("sech,edh->secd", up_delta, w_up, preferred_element_type=jnp.float32)
    input_part = input_part.astype(jnp.bfloat16).reshape(groups * slot_count, slice_d)
    grad_down = jnp.einsum(
        "sech,secd->ehd", hidden_four, grads_four, preferred_element_type=jnp.float32
    ).astype(jnp.bfloat16)
    grad_gate = jnp.einsum(
        "secd,sech->edh", rows_four, gate_delta, preferred_element_type=jnp.float32
    ).astype(jnp.bfloat16)
    grad_up = jnp.einsum(
        "secd,sech->edh", rows_four, up_delta, preferred_element_type=jnp.float32
    ).astype(jnp.bfloat16)
    out_rows, input_rows = (
        lax.all_to_all(expert_out, "dp", split_axis=0, concat_axis=1, tiled=True),
        lax.all_to_all(input_part, "dp", split_axis=0, concat_axis=1, tiled=True),
    )
    out_float = out_rows.astype(jnp.float32)
    scores = jnp.sum(grad_rows * out_float, 1)
    prob_part = jnp.dot(select.T, scores, precision=lax.Precision.HIGHEST).reshape(tok_g, fan_out)
    mix_table = (per_token * weights[:, None]).T
    mixed_part = jnp.dot(mix_table, out_float, precision=lax.Precision.HIGHEST)
    input_sum = jnp.dot(token_pick.T, input_rows, preferred_element_type=jnp.float32)
    mixed_block, input_block = (
        lax.psum_scatter(
            mixed_part.astype(jnp.bfloat16), "expert", scatter_dimension=1, tiled=True
        ).astype(jnp.float32),
        lax.psum_scatter(
            input_sum.astype(jnp.bfloat16), "expert", scatter_dimension=1, tiled=True
        ).astype(jnp.float32),
    )
    mixed, input_grad = (
        lax.all_gather(mixed_block.astype(jnp.bfloat16), "expert", axis=1, tiled=True),
        lax.all_gather(input_block.astype(jnp.bfloat16), "expert", axis=1, tiled=True),
    )
    prob_grad = lax.psum(prob_part, "expert")
    return (mixed, input_grad, prob_grad, grad_gate, grad_up, grad_down)


MESH = pl.DeviceIdType.MESH
F32, BF16 = jnp.float32, jnp.bfloat16
DP, EP = 4, 8
ROWS = 32
AHEAD = 2
LAG = 2


def place():
    z, e = lax.axis_index("dp"), lax.axis_index("expert")
    core, chip = lax.rem(e, 2), lax.div(e, 2)
    x, y = lax.rem(chip, 2), lax.div(chip, 2)
    across = [y * 2 + (1 - x), (1 - y) * 2 + x, (1 - y) * 2 + (1 - x)]
    return z, e, core, chip, across


def lanes(start, size):
    return pl.ds(pl.multiple_of(start, 128), size)


def rows_at(start, size):
    return pl.ds(pl.multiple_of(start, 32), size)


def greet(peers):
    barrier = pltpu.get_barrier_semaphore()
    for peer in peers:
        pl.semaphore_signal(barrier, inc=1, device_id=peer, device_id_type=MESH)
    pl.semaphore_wait(barrier, len(peers))


def push(src, dst, send, recv, peer):
    return pltpu.make_async_remote_copy(
        src_ref=src, dst_ref=dst, send_sem=send, recv_sem=recv, device_id=peer, device_id_type=MESH
    )


def spread_kernel(tok, grad, info, both, infos, s1, r1, s2, r2, s3, r3):
    z, e, core, chip, across = place()
    tok_g, total = tok.shape[0], tok.shape[0] * DP
    block = tok.shape[1] // DP
    part = block // EP
    sibling = chip * 2 + (1 - core)
    peers = [(lax.rem(z + k, DP), e) for k in (1, 2, 3)]
    greet(peers + [(z, sibling)] + [(z, c * 2 + core) for c in across])
    mine = lanes(e * part, part)
    sent, first = [], []
    for k, peer in enumerate(peers):
        for a, src in enumerate((tok, grad)):
            first.append(
                push(
                    src.at[:, lanes(peer[0] * block + e * part, part)],
                    both.at[rows_at(a * total + z * tok_g, tok_g), mine],
                    s1.at[a, k],
                    r1.at[a, k],
                    peer,
                )
            )
        first.append(push(info, infos.at[z], s1.at[2, k], r1.at[2, k], peer))
    for copy in first:
        copy.start()
    for a, src in enumerate((tok, grad)):
        both[rows_at(a * total + z * tok_g, tok_g), mine] = src[
            :, lanes(z * block + e * part, part)
        ]
    infos[z] = info[...]
    for copy in first:
        copy.wait_recv()
    second = [
        push(both.at[:, mine], both.at[:, mine], s2.at[j], r2.at[j], (z, c * 2 + core))
        for j, c in enumerate(across)
    ]
    for copy in second:
        copy.start()
    third = [push(both.at[:, mine], both.at[:, mine], s3.at[0], r3.at[0], (z, sibling))]
    third[0].start()
    for j, c in enumerate(across):
        second[j].wait_recv()
        theirs = lanes((c * 2 + core) * part, part)
        third.append(
            push(
                both.at[:, theirs], both.at[:, theirs], s3.at[j + 1], r3.at[j + 1], (z, sibling)
            )
        )
        third[-1].start()
    for copy in third:
        copy.wait_recv()
    for copy in first + second + third:
        copy.wait_send()


def hidden_kernel(part, out, got, summed, s1, r1, s2, r2):
    z, e = lax.axis_index("dp"), lax.axis_index("expert")
    half = part.shape[0] // 2
    width = part.shape[1] // 3
    steps = half // ROWS
    barrier = pltpu.get_barrier_semaphore()
    inner = (z > 0) & (z < DP - 1)

    @pl.when(z > 0)
    def _():
        pl.semaphore_signal(barrier, inc=1, device_id=(z - 1, e), device_id_type=MESH)

    @pl.when(z < DP - 1)
    def _():
        pl.semaphore_signal(barrier, inc=1, device_id=(z + 1, e), device_id_type=MESH)

    @pl.when(inner)
    def _():
        pl.semaphore_wait(barrier, 2)

    @pl.when(jnp.logical_not(inner))
    def _():
        pl.semaphore_wait(barrier, 1)

    def onward(d):
        return (z + 1, e) if d == 0 else (z - 1, e)

    def backward(d):
        return (z - 1, e) if d == 0 else (z + 1, e)

    def spot(d, c):
        return rows_at(d * half + c * ROWS, ROWS)

    def fan_in(d, c, src):
        return push(src, got.at[d, c], s1.at[d, c], r1.at[d, c], onward(d))

    def fan_out(d, c):
        rows = spot(d, c)
        return push(out.at[rows], out.at[rows], s2.at[d, c], r2.at[d, c], backward(d))

    first = [z == 0, z == DP - 1]
    last = [z == DP - 1, z == 0]

    def feed(c, carry):
        for d in (0, 1):

            @pl.when(first[d] & (c >= AHEAD))
            def _():
                fan_in(d, c - AHEAD, part.at[spot(d, c - AHEAD)]).wait_send()

            @pl.when(first[d])
            def _():
                fan_in(d, c, part.at[spot(d, c)]).start()

        return carry

    lax.fori_loop(0, steps, feed, 0)

    def gather(t, carry):
        for d in (0, 1):
            c = t - LAG * (z if d == 0 else DP - 1 - z)
            live = (c >= 0) & (c < steps)

            @pl.when(inner & live)
            def _():
                fan_in(d, c, summed.at[d, c]).wait_recv()
                total = got[d, c].astype(F32) + part[spot(d, c), :].astype(F32)
                summed[d, c] = total.astype(BF16)
                fan_in(d, c, summed.at[d, c]).start()

            @pl.when(last[d] & live)
            def _():
                fan_in(d, c, summed.at[d, c]).wait_recv()
                total = got[d, c].astype(F32) + part[spot(d, c), :].astype(F32)
                gate = total[:, :width]
                up = total[:, width : 2 * width]
                back = total[:, 2 * width :]
                sig = jax.nn.sigmoid(gate)
                act = gate * sig
                rows = spot(d, c)
                out[rows, 0:width] = (act * up).astype(BF16)
                out[rows, width : 2 * width] = (
                    back * up * sig * (1.0 + gate * (1.0 - sig))
                ).astype(BF16)
                out[rows, 2 * width : 3 * width] = (back * act).astype(BF16)

            @pl.when(last[d] & (c >= AHEAD) & live)
            def _():
                fan_out(d, c - AHEAD).wait_send()

            @pl.when(last[d] & live)
            def _():
                fan_out(d, c).start()

        return carry

    lax.fori_loop(0, steps + LAG * (DP - 1), gather, 0)

    def relay(t, carry):
        for d in (0, 1):
            c = t - LAG * (DP - 1 - z if d == 0 else z)
            live = (c >= 0) & (c < steps)

            @pl.when(inner & live)
            def _():
                fan_out(d, c).wait_recv()
                fan_out(d, c).start()

        return carry

    lax.fori_loop(0, steps + LAG * (DP - 1), relay, 0)

    def finish(c, carry):
        for d in (0, 1):

            @pl.when(first[d])
            def _():
                fan_out(d, c).wait_recv()

            @pl.when(first[d] & (c >= steps - AHEAD))
            def _():
                fan_in(d, c, part.at[spot(d, c)]).wait_send()

            @pl.when(inner)
            def _():
                fan_in(d, c, summed.at[d, c]).wait_send()
                fan_out(d, c).wait_send()

            @pl.when(last[d] & (c >= steps - AHEAD))
            def _():
                fan_out(d, c).wait_send()

        return carry

    lax.fori_loop(0, steps, finish, 0)


def collect_kernel(
    part, prob_part, mixed, inp, prob, near, sums, far, own, table, zprob, eprob,
    s1, r1, s2, r2, s3, r3, s4, r4, s5, r5, s6, r6, s7, r7,
):
    z, e, core, chip, across = place()
    tok_g, total = mixed.shape[0], mixed.shape[0] * DP
    block = part.shape[1]
    width = block // EP
    sibling = chip * 2 + (1 - core)
    zpeers = [(lax.rem(z + k, DP), e) for k in (1, 2, 3)]
    epeers = [(z, lax.rem(e + i, EP)) for i in range(1, EP)]
    greet(zpeers + epeers)
    done = []
    near_in = []
    order = across + [chip]
    for i, c in enumerate(order):
        copy = push(
            part.at[:, lanes((c * 2 + 1 - core) * width, width)],
            near.at[c],
            s1.at[i],
            r1.at[i],
            (z, sibling),
        )
        copy.start()
        near_in.append(copy)
    prob_in = []
    for k, peer in enumerate(zpeers):
        copy = push(prob_part.at[peer[0]], zprob.at[k], s6.at[k], r6.at[k], peer)
        copy.start()
        prob_in.append(copy)
    far_in = []
    for i, c in enumerate(across):
        near_in[i].wait_recv()
        sums[c] = (
            part[:, lanes((c * 2 + core) * width, width)].astype(F32) + near[c].astype(F32)
        ).astype(BF16)
        copy = push(sums.at[c], far.at[i], s2.at[i], r2.at[i], (z, c * 2 + core))
        copy.start()
        far_in.append(copy)
    for copy in prob_in:
        copy.wait_recv()
    eprob[e] = prob_part[z] + zprob[0] + zprob[1] + zprob[2]
    prob_out = []
    for i, peer in enumerate(epeers):
        copy = push(eprob.at[e], eprob.at[e], s7.at[i], r7.at[i], peer)
        copy.start()
        prob_out.append(copy)
    near_in[3].wait_recv()
    for copy in far_in:
        copy.wait_recv()
    own[...] = (
        part[:, lanes(e * width, width)].astype(F32)
        + near[chip].astype(F32)
        + far[0].astype(F32)
        + far[1].astype(F32)
        + far[2].astype(F32)
    ).astype(BF16)
    home = []
    for k, peer in enumerate(zpeers):
        for a in (0, 1):
            copy = push(
                own.at[rows_at(a * total + peer[0] * tok_g, tok_g)],
                table.at[e, pl.ds(a * tok_g, tok_g), lanes(z * width, width)],
                s3.at[a, k],
                r3.at[a, k],
                peer,
            )
            copy.start()
            home.append(copy)
    for a in (0, 1):
        table[e, pl.ds(a * tok_g, tok_g), lanes(z * width, width)] = own[
            rows_at(a * total + z * tok_g, tok_g)
        ]
    for copy in home:
        copy.wait_recv()
    wide = [
        push(table.at[e], table.at[e], s4.at[i], r4.at[i], (z, c * 2 + core))
        for i, c in enumerate(across)
    ]
    pair = [push(table.at[e], table.at[e], s5.at[0], r5.at[0], (z, sibling))]
    for copy in wide + pair:
        copy.start()
    for i, c in enumerate(across):
        wide[i].wait_recv()
        there = c * 2 + core
        copy = push(table.at[there], table.at[there], s5.at[i + 1], r5.at[i + 1], (z, sibling))
        copy.start()
        pair.append(copy)
    for copy in prob_out:
        copy.wait_recv()
    prob[...] = jnp.sum(eprob[...], axis=0)
    for copy in pair:
        copy.wait_recv()
    for q in range(EP):
        for b in range(DP):
            at = slice(b * block + q * width, b * block + (q + 1) * width)
            mixed[:, at] = table[q, 0:tok_g, b * width : (b + 1) * width]
            inp[:, at] = table[q, tok_g : 2 * tok_g, b * width : (b + 1) * width]
    for copy in near_in + prob_in + far_in + prob_out + home + wide + pair:
        copy.wait_send()


def vmem():
    return pl.BlockSpec(memory_space=pltpu.VMEM)


def sems(*shapes):
    return [pltpu.SemaphoreType.DMA(s) for s in shapes for _ in (0, 1)]


def params(number):
    return pltpu.CompilerParams(
        collective_id=number, has_side_effects=True, vmem_limit_bytes=40 * 2**20
    )


def shards(tokens, routes, route_probs, w_gate, w_up, w_down, out_grad):
    tok_g, fan_out = routes.shape
    exp_dev, slice_d, hidden = w_gate.shape
    experts = exp_dev * EP
    capacity = min(tok_g, max(2, 5 * tok_g * fan_out // (4 * experts)))
    total, feats = tok_g * DP, tokens.shape[1]
    owner = lax.axis_index("expert")
    info = jnp.concatenate([routes.astype(F32), route_probs], 1).T
    both, infos = pl.pallas_call(
        spread_kernel,
        out_shape=(
            jax.ShapeDtypeStruct((2 * total, slice_d), BF16),
            jax.ShapeDtypeStruct((DP,) + info.shape, F32),
        ),
        in_specs=[vmem()] * 3,
        out_specs=(vmem(), vmem()),
        scratch_shapes=sems((3, 3), (3,), (4,)),
        compiler_params=params(0),
        name="spread",
    )(tokens, out_grad, info)
    ids = infos[:, :fan_out].astype(jnp.int32)
    probs = infos[:, fan_out:]
    local = owner * exp_dev + jnp.arange(exp_dev, dtype=jnp.int32)
    named = (ids[None] == local[:, None, None, None]).astype(F32)
    member = jnp.sum(named, 2)
    weight = jnp.sum(named * probs[None], 2)
    earlier = jnp.arange(tok_g)[:, None] < jnp.arange(tok_g)[None, :]
    rank = jnp.einsum(
        "egt,tu->egu", member.astype(BF16), earlier.astype(BF16), preferred_element_type=F32
    )
    chosen = (rank[:, :, None, :] == jnp.arange(capacity, dtype=F32)[:, None]) & (
        member[:, :, None, :] > 0
    )
    pick = chosen.astype(BF16)
    slot_weight = jnp.sum(jnp.where(chosen, weight[:, :, None, :], 0.0), 3)
    parts = both.reshape(2, DP, tok_g, slice_d)
    rows = jnp.einsum("egct,gtd->egcd", pick, parts[0], preferred_element_type=F32)
    rows = rows.astype(BF16).reshape(exp_dev, DP * capacity, slice_d)
    grad_rows = jnp.einsum("egct,gtd->egcd", pick, parts[1], preferred_element_type=F32)
    grads = (slot_weight[..., None] * grad_rows).astype(BF16)
    grads = grads.reshape(exp_dev, DP * capacity, slice_d)
    gate_part = jnp.einsum("erd,edh->erh", rows, w_gate, preferred_element_type=F32)
    up_part = jnp.einsum("erd,edh->erh", rows, w_up, preferred_element_type=F32)
    back_part = jnp.einsum("erd,ehd->erh", grads, w_down, preferred_element_type=F32)
    part = jnp.concatenate(
        [gate_part.astype(BF16), up_part.astype(BF16), back_part.astype(BF16)], 2
    ).reshape(exp_dev * DP * capacity, 3 * hidden)
    steps = part.shape[0] // 2 // ROWS
    full = pl.pallas_call(
        hidden_kernel,
        out_shape=jax.ShapeDtypeStruct(part.shape, BF16),
        in_specs=[vmem()],
        out_specs=vmem(),
        scratch_shapes=[
            pltpu.VMEM((2, steps, ROWS, 3 * hidden), BF16),
            pltpu.VMEM((2, steps, ROWS, 3 * hidden), BF16),
        ]
        + sems((2, steps), (2, steps)),
        compiler_params=params(1),
        name="hidden",
    )(part)
    full = full.reshape(exp_dev, DP * capacity, 3 * hidden)
    hid = full[..., :hidden]
    d_gate = full[..., hidden : 2 * hidden]
    d_up = full[..., 2 * hidden :]
    outs = jnp.einsum("erh,ehd->erd", hid, w_down, preferred_element_type=F32)
    outs = outs.reshape(exp_dev, DP, capacity, slice_d)
    inputs = jnp.einsum("erh,edh->erd", d_gate, w_gate, preferred_element_type=F32) + jnp.einsum(
        "erh,edh->erd", d_up, w_up, preferred_element_type=F32
    )
    inputs = inputs.astype(BF16).reshape(exp_dev, DP, capacity, slice_d)
    scores = jnp.sum(grad_rows * outs, 3)
    by_token = jnp.sum(jnp.where(chosen, scores[..., None], 0.0), 2)
    prob_part = jnp.sum(named * by_token[:, :, None, :], 0)
    scaled = (slot_weight[..., None] * outs).astype(BF16)
    mixed_part = jnp.einsum("egct,egcd->gtd", pick, scaled, preferred_element_type=F32)
    input_sum = jnp.einsum("egct,egcd->gtd", pick, inputs, preferred_element_type=F32)
    packed = jnp.concatenate([mixed_part.astype(BF16), input_sum.astype(BF16)], 0)
    packed = packed.reshape(2 * total, slice_d)
    width = slice_d // EP
    mixed, input_grad, prob = pl.pallas_call(
        collect_kernel,
        out_shape=(
            jax.ShapeDtypeStruct((tok_g, feats), BF16),
            jax.ShapeDtypeStruct((tok_g, feats), BF16),
            jax.ShapeDtypeStruct((fan_out, tok_g), F32),
        ),
        in_specs=[vmem()] * 2,
        out_specs=(vmem(), vmem(), vmem()),
        scratch_shapes=[
            pltpu.VMEM((4, 2 * total, width), BF16),
            pltpu.VMEM((4, 2 * total, width), BF16),
            pltpu.VMEM((3, 2 * total, width), BF16),
            pltpu.VMEM((2 * total, width), BF16),
            pltpu.VMEM((EP, 2 * tok_g, DP * width), BF16),
            pltpu.VMEM((3, fan_out, tok_g), F32),
            pltpu.VMEM((EP, fan_out, tok_g), F32),
        ]
        + sems((4,), (3,), (2, 3), (3,), (4,), (3,), (7,)),
        compiler_params=params(2),
        name="collect",
    )(packed, prob_part)
    grad_down = jnp.einsum("erh,erd->ehd", hid, grads, preferred_element_type=F32).astype(BF16)
    grad_gate = jnp.einsum("erd,erh->edh", rows, d_gate, preferred_element_type=F32).astype(BF16)
    grad_up = jnp.einsum("erd,erh->edh", rows, d_up, preferred_element_type=F32).astype(BF16)
    return (mixed, input_grad, prob.T, grad_gate, grad_up, grad_down)


def solution(mesh):
    in_specs = (
        P("dp", None),
        P("dp", None),
        P("dp", None),
        P("expert", "dp", None),
        P("expert", "dp", None),
        P("expert", None, "dp"),
        P("dp", None),
    )
    out_specs = (
        P("dp", None),
        P("dp", None),
        P("dp", None),
        P("expert", "dp", None),
        P("expert", "dp", None),
        P("expert", None, "dp"),
    )
    body = shards if (mesh.shape["dp"], mesh.shape["expert"]) == (DP, EP) else plain_shards
    return jax.shard_map(body, mesh=mesh, in_specs=in_specs, out_specs=out_specs, check_vma=False)
```

```python
import jax
import jax.numpy as jnp
from jax import lax
from jax.experimental import pallas as pl
from jax.experimental.pallas import tpu as pltpu
from jax.sharding import PartitionSpec as P


def plain_shards(tokens, routes, route_probs, w_gate, w_up, w_down, out_grad):
    tok_g, fan_out = routes.shape
    exp_dev, slice_d, hidden = w_gate.shape
    experts = exp_dev * lax.axis_size("expert")
    capacity = min(tok_g, max(2, 5 * tok_g * fan_out // (4 * experts)))
    slot_count = exp_dev * capacity
    owner_index = lax.axis_index("expert")
    flat_ids = routes.reshape(-1)
    onehot = (flat_ids[:, None] == jnp.arange(experts, dtype=jnp.int32)[None, :]).astype(jnp.int32)
    slot_rank = jnp.sum((jnp.cumsum(onehot, 0) - onehot) * onehot, 1)
    local_id = flat_ids - owner_index * exp_dev
    target = jnp.where((local_id >= 0) & (local_id < exp_dev), local_id * capacity + slot_rank, -1)
    select = (jnp.arange(slot_count, dtype=jnp.int32)[:, None] == target[None, :]).astype(
        jnp.float32
    )
    per_token = jnp.sum(select.reshape(slot_count, tok_g, fan_out), 2)
    weights = jnp.dot(select, route_probs.reshape(-1), precision=lax.Precision.HIGHEST)
    token_pick = per_token.astype(jnp.bfloat16)
    sent_rows = jnp.dot(token_pick, tokens, preferred_element_type=jnp.float32).astype(jnp.bfloat16)
    grad_rows = jnp.dot(token_pick, out_grad, preferred_element_type=jnp.float32)
    grad_sent = (weights[:, None] * grad_rows).astype(jnp.bfloat16)
    all_rows, all_grads = (
        lax.all_to_all(sent_rows, "dp", split_axis=1, concat_axis=0, tiled=True),
        lax.all_to_all(grad_sent, "dp", split_axis=1, concat_axis=0, tiled=True),
    )
    groups = all_rows.shape[0] // slot_count
    part_rows = all_rows.reshape(
        slot_count * lax.axis_size("dp") // slot_count, exp_dev, capacity, slice_d
    )
    part_grads = all_grads.reshape(
        slot_count * lax.axis_size("dp") // slot_count, exp_dev, capacity, slice_d
    )
    gate_part = jnp.einsum("secd,edh->sech", part_rows, w_gate, preferred_element_type=jnp.float32)
    up_part = jnp.einsum("secd,edh->sech", part_rows, w_up, preferred_element_type=jnp.float32)
    back_part = jnp.einsum("secd,ehd->sech", part_grads, w_down, preferred_element_type=jnp.float32)
    reduced = lax.psum_scatter(
        jnp.concatenate([gate_part, up_part, back_part], 3)
        .reshape(slot_count * lax.axis_size("dp"), 3 * hidden)
        .astype(jnp.bfloat16),
        "dp",
        scatter_dimension=0,
        tiled=True,
    ).astype(jnp.float32)
    gate_sum = reduced[:, :hidden]
    up_sum = reduced[:, hidden : 2 * hidden]
    back_sum = reduced[:, 2 * hidden :]
    gate_sig = jax.nn.sigmoid(gate_sum)
    activated = gate_sum * gate_sig
    hidden_rows = (activated * up_sum).astype(jnp.bfloat16)
    delta_gate = (back_sum * up_sum * gate_sig * (1.0 + gate_sum * (1.0 - gate_sig))).astype(
        jnp.bfloat16
    )
    delta_up = (back_sum * activated).astype(jnp.bfloat16)
    all_hidden, all_delta = (
        lax.all_gather(hidden_rows, "dp", axis=0, tiled=True),
        lax.all_gather(jnp.concatenate([delta_gate, delta_up], 1), "dp", axis=0, tiled=True),
    )
    hidden_four = all_hidden.reshape(groups, exp_dev, capacity, hidden)
    delta_four = all_delta.reshape(groups, exp_dev, capacity, 2 * hidden)
    rows_four = all_rows.reshape(groups, exp_dev, capacity, slice_d)
    grads_four = all_grads.reshape(groups, exp_dev, capacity, slice_d)
    gate_delta = delta_four[..., :hidden]
    up_delta = delta_four[..., hidden:]
    expert_out = jnp.einsum(
        "sech,ehd->secd", hidden_four, w_down, preferred_element_type=jnp.float32
    )
    expert_out = expert_out.astype(jnp.bfloat16).reshape(groups * slot_count, slice_d)
    input_part = jnp.einsum(
        "sech,edh->secd", gate_delta, w_gate, preferred_element_type=jnp.float32
    ) + jnp.einsum("sech,edh->secd", up_delta, w_up, preferred_element_type=jnp.float32)
    input_part = input_part.astype(jnp.bfloat16).reshape(groups * slot_count, slice_d)
    grad_down = jnp.einsum(
        "sech,secd->ehd", hidden_four, grads_four, preferred_element_type=jnp.float32
    ).astype(jnp.bfloat16)
    grad_gate = jnp.einsum(
        "secd,sech->edh", rows_four, gate_delta, preferred_element_type=jnp.float32
    ).astype(jnp.bfloat16)
    grad_up = jnp.einsum(
        "secd,sech->edh", rows_four, up_delta, preferred_element_type=jnp.float32
    ).astype(jnp.bfloat16)
    out_rows, input_rows = (
        lax.all_to_all(expert_out, "dp", split_axis=0, concat_axis=1, tiled=True),
        lax.all_to_all(input_part, "dp", split_axis=0, concat_axis=1, tiled=True),
    )
    out_float = out_rows.astype(jnp.float32)
    scores = jnp.sum(grad_rows * out_float, 1)
    prob_part = jnp.dot(select.T, scores, precision=lax.Precision.HIGHEST).reshape(tok_g, fan_out)
    mix_table = (per_token * weights[:, None]).T
    mixed_part = jnp.dot(mix_table, out_float, precision=lax.Precision.HIGHEST)
    input_sum = jnp.dot(token_pick.T, input_rows, preferred_element_type=jnp.float32)
    mixed_block, input_block = (
        lax.psum_scatter(
            mixed_part.astype(jnp.bfloat16), "expert", scatter_dimension=1, tiled=True
        ).astype(jnp.float32),
        lax.psum_scatter(
            input_sum.astype(jnp.bfloat16), "expert", scatter_dimension=1, tiled=True
        ).astype(jnp.float32),
    )
    mixed, input_grad = (
        lax.all_gather(mixed_block.astype(jnp.bfloat16), "expert", axis=1, tiled=True),
        lax.all_gather(input_block.astype(jnp.bfloat16), "expert", axis=1, tiled=True),
    )
    prob_grad = lax.psum(prob_part, "expert")
    return (mixed, input_grad, prob_grad, grad_gate, grad_up, grad_down)


MESH = pl.DeviceIdType.MESH
F32, BF16 = jnp.float32, jnp.bfloat16
DP, EP = 4, 8
ROWS = 16
AHEAD = 3
LAG = 3


def place():
    z, e = lax.axis_index("dp"), lax.axis_index("expert")
    core, chip = lax.rem(e, 2), lax.div(e, 2)
    x, y = lax.rem(chip, 2), lax.div(chip, 2)
    across = [y * 2 + (1 - x), (1 - y) * 2 + x, (1 - y) * 2 + (1 - x)]
    return z, e, core, chip, across


def lanes(start, size):
    return pl.ds(pl.multiple_of(start, 128), size)


def rows_at(start, size):
    return pl.ds(pl.multiple_of(start, 16), size)


def greet(peers):
    barrier = pltpu.get_barrier_semaphore()
    for peer in peers:
        pl.semaphore_signal(barrier, inc=1, device_id=peer, device_id_type=MESH)
    pl.semaphore_wait(barrier, len(peers))


def push(src, dst, send, recv, peer):
    return pltpu.make_async_remote_copy(
        src_ref=src, dst_ref=dst, send_sem=send, recv_sem=recv, device_id=peer, device_id_type=MESH
    )


def spread_kernel(tok, grad, info, both, infos, s1, r1, s2, r2, s3, r3):
    z, e, core, chip, across = place()
    tok_g, total = tok.shape[0], tok.shape[0] * DP
    block = tok.shape[1] // DP
    part = block // EP
    sibling = chip * 2 + (1 - core)
    peers = [(lax.rem(z + k, DP), e) for k in (1, 2, 3)]
    greet(peers + [(z, sibling)] + [(z, c * 2 + core) for c in across])
    mine = lanes(e * part, part)
    notes, first = [], []
    for k, peer in enumerate(peers):
        for a, src in enumerate((tok, grad)):
            first.append(
                push(
                    src.at[:, lanes(peer[0] * block + e * part, part)],
                    both.at[rows_at(a * total + z * tok_g, tok_g), mine],
                    s1.at[a, k],
                    r1.at[a, k],
                    peer,
                )
            )
        notes.append(push(info, infos.at[z], s1.at[2, k], r1.at[2, k], peer))
    for copy in first[0::2] + first[1::2] + notes:
        copy.start()
    for a, src in enumerate((tok, grad)):
        both[rows_at(a * total + z * tok_g, tok_g), mine] = src[
            :, lanes(z * block + e * part, part)
        ]
    infos[z] = info[...]
    second, third = [], []
    for a in (0, 1):
        half = pl.ds(a * total, total)
        for k in range(3):
            first[k * 2 + a].wait_recv()
        block_a = both.at[half, mine]
        for j, c in enumerate(across):
            second.append(push(block_a, block_a, s2.at[a, j], r2.at[a, j], (z, c * 2 + core)))
            second[-1].start()
        third.append(push(block_a, block_a, s3.at[a, 0], r3.at[a, 0], (z, sibling)))
        third[-1].start()
    for a in (0, 1):
        half = pl.ds(a * total, total)
        for j, c in enumerate(across):
            second[a * 3 + j].wait_recv()
            theirs = both.at[half, lanes((c * 2 + core) * part, part)]
            third.append(push(theirs, theirs, s3.at[a, j + 1], r3.at[a, j + 1], (z, sibling)))
            third[-1].start()
    for k in range(3):
        notes[k].wait_recv()
    for copy in third:
        copy.wait_recv()
    first = first + notes
    for copy in first + second + third:
        copy.wait_send()


def hidden_kernel(part, out, got, summed, s1, r1, s2, r2):
    z, e = lax.axis_index("dp"), lax.axis_index("expert")
    half = part.shape[0] // 2
    width = part.shape[1] // 3
    steps = half // ROWS
    barrier = pltpu.get_barrier_semaphore()
    inner = (z > 0) & (z < DP - 1)

    @pl.when(z > 0)
    def _():
        pl.semaphore_signal(barrier, inc=1, device_id=(z - 1, e), device_id_type=MESH)

    @pl.when(z < DP - 1)
    def _():
        pl.semaphore_signal(barrier, inc=1, device_id=(z + 1, e), device_id_type=MESH)

    @pl.when(inner)
    def _():
        pl.semaphore_wait(barrier, 2)

    @pl.when(jnp.logical_not(inner))
    def _():
        pl.semaphore_wait(barrier, 1)

    def onward(d):
        return (z + 1, e) if d == 0 else (z - 1, e)

    def backward(d):
        return (z - 1, e) if d == 0 else (z + 1, e)

    def spot(d, c):
        return rows_at(d * half + c * ROWS, ROWS)

    def fan_in(d, c, src):
        return push(src, got.at[d, c], s1.at[d, c], r1.at[d, c], onward(d))

    def fan_out(d, c):
        rows = spot(d, c)
        return push(out.at[rows], out.at[rows], s2.at[d, c], r2.at[d, c], backward(d))

    first = [z == 0, z == DP - 1]
    last = [z == DP - 1, z == 0]

    def feed(c, carry):
        for d in (0, 1):

            @pl.when(first[d] & (c >= AHEAD))
            def _():
                fan_in(d, c - AHEAD, part.at[spot(d, c - AHEAD)]).wait_send()

            @pl.when(first[d])
            def _():
                fan_in(d, c, part.at[spot(d, c)]).start()

        return carry

    lax.fori_loop(0, steps, feed, 0)

    def gather(t, carry):
        for d in (0, 1):
            c = t - LAG * (z if d == 0 else DP - 1 - z)
            live = (c >= 0) & (c < steps)

            @pl.when(inner & live)
            def _():
                fan_in(d, c, summed.at[d, c]).wait_recv()
                total = got[d, c].astype(F32) + part[spot(d, c), :].astype(F32)
                summed[d, c] = total.astype(BF16)
                fan_in(d, c, summed.at[d, c]).start()

            @pl.when(last[d] & live)
            def _():
                fan_in(d, c, summed.at[d, c]).wait_recv()
                total = got[d, c].astype(F32) + part[spot(d, c), :].astype(F32)
                gate = total[:, :width]
                up = total[:, width : 2 * width]
                back = total[:, 2 * width :]
                sig = jax.nn.sigmoid(gate)
                act = gate * sig
                rows = spot(d, c)
                out[rows, 0:width] = (act * up).astype(BF16)
                out[rows, width : 2 * width] = (
                    back * up * sig * (1.0 + gate * (1.0 - sig))
                ).astype(BF16)
                out[rows, 2 * width : 3 * width] = (back * act).astype(BF16)

            @pl.when(last[d] & (c >= AHEAD) & live)
            def _():
                fan_out(d, c - AHEAD).wait_send()

            @pl.when(last[d] & live)
            def _():
                fan_out(d, c).start()

        return carry

    lax.fori_loop(0, steps + LAG * (DP - 1), gather, 0)

    def relay(t, carry):
        for d in (0, 1):
            c = t - LAG * (DP - 1 - z if d == 0 else z)
            live = (c >= 0) & (c < steps)

            @pl.when(inner & live)
            def _():
                fan_out(d, c).wait_recv()
                fan_out(d, c).start()

        return carry

    lax.fori_loop(0, steps + LAG * (DP - 1), relay, 0)

    def finish(c, carry):
        for d in (0, 1):

            @pl.when(first[d])
            def _():
                fan_out(d, c).wait_recv()

            @pl.when(first[d] & (c >= steps - AHEAD))
            def _():
                fan_in(d, c, part.at[spot(d, c)]).wait_send()

            @pl.when(inner)
            def _():
                fan_in(d, c, summed.at[d, c]).wait_send()
                fan_out(d, c).wait_send()

            @pl.when(last[d] & (c >= steps - AHEAD))
            def _():
                fan_out(d, c).wait_send()

        return carry

    lax.fori_loop(0, steps, finish, 0)


def collect_kernel(
    part, prob_part, mixed, inp, prob, near, sums, far, own, table, zprob, eprob,
    s1, r1, s2, r2, s3, r3, s4, r4, s5, r5, s6, r6, s7, r7,
):
    z, e, core, chip, across = place()
    tok_g, total = mixed.shape[0], mixed.shape[0] * DP
    block = part.shape[1]
    width = block // EP
    sibling = chip * 2 + (1 - core)
    zpeers = [(lax.rem(z + k, DP), e) for k in (1, 2, 3)]
    epeers = [(z, lax.rem(e + i, EP)) for i in range(1, EP)]
    greet(zpeers + epeers)
    order = across + [chip]
    halves = [pl.ds(0, total), pl.ds(total, total)]
    near_in, far_in, home, wide, pair = [], [], [], [], []
    for a, half in enumerate(halves):
        for i, c in enumerate(order):
            theirs = part.at[half, lanes((c * 2 + 1 - core) * width, width)]
            near_in.append(push(theirs, near.at[c, half], s1.at[a, i], r1.at[a, i], (z, sibling)))
            near_in[-1].start()
    prob_in = []
    for k, peer in enumerate(zpeers):
        prob_in.append(push(prob_part.at[peer[0]], zprob.at[k], s6.at[k], r6.at[k], peer))
        prob_in[-1].start()
    for a, half in enumerate(halves):
        for i, c in enumerate(across):
            near_in[a * 4 + i].wait_recv()
            sums[c, half] = (
                part[half, lanes((c * 2 + core) * width, width)].astype(F32)
                + near[c, half].astype(F32)
            ).astype(BF16)
            far_in.append(
                push(
                    sums.at[c, half],
                    far.at[i, half],
                    s2.at[a, i],
                    r2.at[a, i],
                    (z, c * 2 + core),
                )
            )
            far_in[-1].start()
    for copy in prob_in:
        copy.wait_recv()
    eprob[e] = prob_part[z] + zprob[0] + zprob[1] + zprob[2]
    prob_out = []
    for i, peer in enumerate(epeers):
        prob_out.append(push(eprob.at[e], eprob.at[e], s7.at[i], r7.at[i], peer))
        prob_out[-1].start()
    for a, half in enumerate(halves):
        near_in[a * 4 + 3].wait_recv()
        for i in range(3):
            far_in[a * 3 + i].wait_recv()
        own[half] = (
            part[half, lanes(e * width, width)].astype(F32)
            + near[chip, half].astype(F32)
            + far[0, half].astype(F32)
            + far[1, half].astype(F32)
            + far[2, half].astype(F32)
        ).astype(BF16)
        for k, peer in enumerate(zpeers):
            home.append(
                push(
                    own.at[rows_at(a * total + peer[0] * tok_g, tok_g)],
                    table.at[e, pl.ds(a * tok_g, tok_g), lanes(z * width, width)],
                    s3.at[a, k],
                    r3.at[a, k],
                    peer,
                )
            )
            home[-1].start()
        table[e, pl.ds(a * tok_g, tok_g), lanes(z * width, width)] = own[
            rows_at(a * total + z * tok_g, tok_g)
        ]
    for a in (0, 1):
        for k in range(3):
            home[a * 3 + k].wait_recv()
        ours = table.at[e, pl.ds(a * tok_g, tok_g)]
        for i, c in enumerate(across):
            wide.append(push(ours, ours, s4.at[a, i], r4.at[a, i], (z, c * 2 + core)))
            wide[-1].start()
        pair.append(push(ours, ours, s5.at[a, 0], r5.at[a, 0], (z, sibling)))
        pair[-1].start()
    for a in (0, 1):
        for i, c in enumerate(across):
            wide[a * 3 + i].wait_recv()
            there = table.at[c * 2 + core, pl.ds(a * tok_g, tok_g)]
            pair.append(push(there, there, s5.at[a, i + 1], r5.at[a, i + 1], (z, sibling)))
            pair[-1].start()
    for copy in prob_out:
        copy.wait_recv()
    prob[...] = jnp.sum(eprob[...], axis=0)
    for copy in pair:
        copy.wait_recv()
    for q in range(EP):
        for b in range(DP):
            at = slice(b * block + q * width, b * block + (q + 1) * width)
            mixed[:, at] = table[q, 0:tok_g, b * width : (b + 1) * width]
            inp[:, at] = table[q, tok_g : 2 * tok_g, b * width : (b + 1) * width]
    for copy in near_in + prob_in + far_in + prob_out + home + wide + pair:
        copy.wait_send()


def vmem():
    return pl.BlockSpec(memory_space=pltpu.VMEM)


def sems(*shapes):
    return [pltpu.SemaphoreType.DMA(s) for s in shapes for _ in (0, 1)]


def params(number):
    return pltpu.CompilerParams(
        collective_id=number, has_side_effects=True, vmem_limit_bytes=40 * 2**20
    )


def shards(tokens, routes, route_probs, w_gate, w_up, w_down, out_grad):
    tok_g, fan_out = routes.shape
    exp_dev, slice_d, hidden = w_gate.shape
    experts = exp_dev * EP
    capacity = min(tok_g, max(2, 5 * tok_g * fan_out // (4 * experts)))
    total, feats = tok_g * DP, tokens.shape[1]
    owner = lax.axis_index("expert")
    info = jnp.concatenate([routes.astype(F32), route_probs], 1).T
    both, infos = pl.pallas_call(
        spread_kernel,
        out_shape=(
            jax.ShapeDtypeStruct((2 * total, slice_d), BF16),
            jax.ShapeDtypeStruct((DP,) + info.shape, F32),
        ),
        in_specs=[vmem()] * 3,
        out_specs=(vmem(), vmem()),
        scratch_shapes=sems((3, 3), (2, 3), (2, 4)),
        compiler_params=params(0),
        name="spread",
    )(tokens, out_grad, info)
    ids = infos[:, :fan_out].astype(jnp.int32)
    probs = infos[:, fan_out:]
    local = owner * exp_dev + jnp.arange(exp_dev, dtype=jnp.int32)
    named = (ids[None] == local[:, None, None, None]).astype(F32)
    member = jnp.sum(named, 2)
    weight = jnp.sum(named * probs[None], 2)
    earlier = jnp.arange(tok_g)[:, None] < jnp.arange(tok_g)[None, :]
    rank = jnp.einsum(
        "egt,tu->egu", member.astype(BF16), earlier.astype(BF16), preferred_element_type=F32
    )
    chosen = (rank[:, :, None, :] == jnp.arange(capacity, dtype=F32)[:, None]) & (
        member[:, :, None, :] > 0
    )
    pick = chosen.astype(BF16)
    slot_weight = jnp.sum(jnp.where(chosen, weight[:, :, None, :], 0.0), 3)
    parts = both.reshape(2, DP, tok_g, slice_d)
    rows = jnp.einsum("egct,gtd->egcd", pick, parts[0], preferred_element_type=F32)
    rows = rows.astype(BF16).reshape(exp_dev, DP * capacity, slice_d)
    grad_rows = jnp.einsum("egct,gtd->egcd", pick, parts[1], preferred_element_type=F32)
    grads = (slot_weight[..., None] * grad_rows).astype(BF16)
    grads = grads.reshape(exp_dev, DP * capacity, slice_d)
    gate_part = jnp.einsum("erd,edh->erh", rows, w_gate, preferred_element_type=F32)
    up_part = jnp.einsum("erd,edh->erh", rows, w_up, preferred_element_type=F32)
    back_part = jnp.einsum("erd,ehd->erh", grads, w_down, preferred_element_type=F32)
    part = jnp.concatenate(
        [gate_part.astype(BF16), up_part.astype(BF16), back_part.astype(BF16)], 2
    ).reshape(exp_dev * DP * capacity, 3 * hidden)
    steps = part.shape[0] // 2 // ROWS
    full = pl.pallas_call(
        hidden_kernel,
        out_shape=jax.ShapeDtypeStruct(part.shape, BF16),
        in_specs=[vmem()],
        out_specs=vmem(),
        scratch_shapes=[
            pltpu.VMEM((2, steps, ROWS, 3 * hidden), BF16),
            pltpu.VMEM((2, steps, ROWS, 3 * hidden), BF16),
        ]
        + sems((2, steps), (2, steps)),
        compiler_params=params(1),
        name="hidden",
    )(part)
    full = full.reshape(exp_dev, DP * capacity, 3 * hidden)
    hid = full[..., :hidden]
    d_gate = full[..., hidden : 2 * hidden]
    d_up = full[..., 2 * hidden :]
    outs = jnp.einsum("erh,ehd->erd", hid, w_down, preferred_element_type=F32)
    outs = outs.reshape(exp_dev, DP, capacity, slice_d)
    inputs = jnp.einsum("erh,edh->erd", d_gate, w_gate, preferred_element_type=F32) + jnp.einsum(
        "erh,edh->erd", d_up, w_up, preferred_element_type=F32
    )
    inputs = inputs.astype(BF16).reshape(exp_dev, DP, capacity, slice_d)
    scores = jnp.sum(grad_rows * outs, 3)
    by_token = jnp.sum(jnp.where(chosen, scores[..., None], 0.0), 2)
    prob_part = jnp.sum(named * by_token[:, :, None, :], 0)
    scaled = (slot_weight[..., None] * outs).astype(BF16)
    mixed_part = jnp.einsum("egct,egcd->gtd", pick, scaled, preferred_element_type=F32)
    input_sum = jnp.einsum("egct,egcd->gtd", pick, inputs, preferred_element_type=F32)
    packed = jnp.concatenate([mixed_part.astype(BF16), input_sum.astype(BF16)], 0)
    packed = packed.reshape(2 * total, slice_d)
    width = slice_d // EP
    mixed, input_grad, prob = pl.pallas_call(
        collect_kernel,
        out_shape=(
            jax.ShapeDtypeStruct((tok_g, feats), BF16),
            jax.ShapeDtypeStruct((tok_g, feats), BF16),
            jax.ShapeDtypeStruct((fan_out, tok_g), F32),
        ),
        in_specs=[vmem()] * 2,
        out_specs=(vmem(), vmem(), vmem()),
        scratch_shapes=[
            pltpu.VMEM((4, 2 * total, width), BF16),
            pltpu.VMEM((4, 2 * total, width), BF16),
            pltpu.VMEM((3, 2 * total, width), BF16),
            pltpu.VMEM((2 * total, width), BF16),
            pltpu.VMEM((EP, 2 * tok_g, DP * width), BF16),
            pltpu.VMEM((3, fan_out, tok_g), F32),
            pltpu.VMEM((EP, fan_out, tok_g), F32),
        ]
        + sems((2, 4), (2, 3), (2, 3), (2, 3), (2, 4), (3,), (7,)),
        compiler_params=params(2),
        name="collect",
    )(packed, prob_part)
    grad_down = jnp.einsum("erh,erd->ehd", hid, grads, preferred_element_type=F32).astype(BF16)
    grad_gate = jnp.einsum("erd,erh->edh", rows, d_gate, preferred_element_type=F32).astype(BF16)
    grad_up = jnp.einsum("erd,erh->edh", rows, d_up, preferred_element_type=F32).astype(BF16)
    return (mixed, input_grad, prob.T, grad_gate, grad_up, grad_down)


def solution(mesh):
    in_specs = (
        P("dp", None),
        P("dp", None),
        P("dp", None),
        P("expert", "dp", None),
        P("expert", "dp", None),
        P("expert", None, "dp"),
        P("dp", None),
    )
    out_specs = (
        P("dp", None),
        P("dp", None),
        P("dp", None),
        P("expert", "dp", None),
        P("expert", "dp", None),
        P("expert", None, "dp"),
    )
    body = shards if (mesh.shape["dp"], mesh.shape["expert"]) == (DP, EP) else plain_shards
    return jax.shard_map(body, mesh=mesh, in_specs=in_specs, out_specs=out_specs, check_vma=False)
```
